32 devices in a mesh: prow: 4 (over y, core), pcol: 8 (over z, x).
Axes of the slice: x: 2, y: 2, z: 4, core: 2. Of those that a mesh axis runs over, the one named last changes fastest.
Arguments:
- factor_rows: float32 [4096, 8192], P('prow', 'pcol'), may hold values from -128 to 128
- measurements: float32 [2048, 8192], P('prow', 'pcol'), may hold values from -256 to 256
- link_blocks: int32 [8, 12], P('prow'), may hold values from 0 to 31, all different within a row
- panel_index: int32 [1], replicated, may hold values from 0 to 30
Outputs:
- reduced_factor: float32 [4096, 8192], P('prow', 'pcol')
- reduced_measurements: float32 [2048, 8192], P('prow', 'pcol')
- panel_row: float32 [256, 8192], P(None, 'pcol')
The draws below stay inside these ranges and needn't reach their ends.
All inputs are finite; a program needn't handle non-finite values.
Results may differ from the reference program's by a relative error of at most 0.0003.
Values sent between devices are 32-bit elements; how exact they have to be, the bound alone decides.
A program may use at most 64 MiB of HBM per device.

```python
import jax
import jax.numpy as jnp
from jax import lax

PB = 256
CB_DEV = 4
TOUCH = 12
CB = 32
COLS = 8192
FROWS = 4096
MBLOCKS = 8
MROWS = 2048
N_PCOL = 8


def row_scales(key, row_count, spread):
    ramp_up = 3.0 ** (jnp.arange(row_count, dtype=jnp.float32) / row_count)
    jitter = jax.random.uniform(key, (row_count,), jnp.float32, -0.5, 0.5)
    return ramp_up * jnp.exp(jitter * jnp.log(spread))


def column_scales(key, col_count):
    jitter = jax.random.uniform(key, (col_count,), jnp.float32, -0.5, 0.5)
    return jnp.exp(jitter * jnp.log(10.0))


def draw_factor_rows(key, part):
    key = jax.random.fold_in(key, 11)
    key_noise, key_rows, key_cols = jax.random.split(key, 3)
    entries = jax.random.truncated_normal(key_noise, -4.0, 4.0, (FROWS, COLS), jnp.float32)
    scales = row_scales(key_rows, FROWS, 10.0)
    return entries * scales[:, None] * column_scales(key_cols, COLS)[None, :]


def draw_measurements(key, part):
    key = jax.random.fold_in(key, 23)
    key_noise, key_rows, key_cols = jax.random.split(key, 3)
    entries = jax.random.truncated_normal(key_noise, -4.0, 4.0, (MROWS, COLS), jnp.float32)
    scales = row_scales(key_rows, MROWS, 10.0)
    return 2.0 * entries * scales[:, None] * column_scales(key_cols, COLS)[None, :]


def distinct(stream_key, rows, count, top, lift):
    ranking = jax.random.permutation(jax.random.fold_in(stream_key, 1), count)
    pull = ranking
    for power in range(3):
        pull = pull * pull // count
    pull = pull * lift // count
    chance = jax.random.randint(jax.random.fold_in(stream_key, 2), (rows, count), 0, 4096) + pull
    holders = jax.random.permutation(jax.random.fold_in(stream_key, 3), rows)[jnp.arange(count) % rows]
    chance = jnp.where(jnp.arange(rows)[:, None] == holders[None, :], 1 << 14, chance)
    priority = chance * count + jnp.arange(count)
    return lax.top_k(priority.astype(jnp.int32), top)[1].astype(jnp.int32)


def setup_inputs(seed: int = 0) -> dict:
    keys = jax.random.split(jax.random.key(seed), 5)
    factor_rows = draw_factor_rows(jax.random.fold_in(keys[4], 71), 0)
    measurements = draw_measurements(jax.random.fold_in(keys[4], 71), 0)
    link_blocks = distinct(keys[2], MBLOCKS, CB, TOUCH, 3072)
    panel_index = jax.random.randint(keys[3], (1,), 0, CB - 1).astype(jnp.int32)
    return {"factor_rows": factor_rows, "measurements": measurements, "link_blocks": link_blocks, "panel_index": panel_index}


highest = lax.Precision.HIGHEST

def cholesky_lower(gram_matrix):
    order = gram_matrix.shape[0]
    index_row = jnp.arange(order, dtype=jnp.int32)

    def one_column(j, carry):
        current, lower_out = carry
        onehot = (index_row == j).astype(current.dtype)
        column = lax.optimization_barrier(jnp.sum(current * onehot[None, :], axis=1))
        pivot = jnp.sum(column * onehot)
        scaled = jnp.where(index_row >= j, column / jnp.sqrt(pivot), jnp.zeros_like(column))
        current = current - scaled[:, None] * scaled[None, :]
        lower_out = lower_out + scaled[:, None] * onehot[None, :]
        return (current, lower_out)
    zeros = jnp.zeros_like(gram_matrix)
    return lax.fori_loop(jnp.int32(0), jnp.int32(order), one_column, (gram_matrix, zeros))[1]

def invert_lower(lower_factor):
    order = lower_factor.shape[0]
    index_row = jnp.arange(order, dtype=jnp.int32)

    def one_row(i, inverse_out):
        onehot = (index_row == i).astype(lower_factor.dtype)
        row_vals = lax.optimization_barrier(jnp.sum(lower_factor * onehot[:, None], axis=0))
        pivot = jnp.sum(row_vals * onehot)
        below = jnp.where(index_row < i, row_vals, jnp.zeros_like(row_vals))
        new_row = (onehot - jnp.dot(below, inverse_out, precision=highest)) / pivot
        return inverse_out + onehot[:, None] * new_row[None, :]
    return lax.fori_loop(jnp.int32(0), jnp.int32(order), one_row, jnp.zeros_like(lower_factor))

def reference(factor_rows, measurements, link_blocks, panel_index):
    block_count = CB_DEV * N_PCOL
    position = jnp.arange(block_count, dtype=jnp.int32)
    blocks = position % CB_DEV * N_PCOL + position // CB_DEV
    touched = jnp.any(link_blocks[:, :, None] == blocks[None, None, :], axis=1)
    keep_rows = jnp.repeat(touched, PB, axis=0)
    target = panel_index[0].astype(jnp.int32)
    panel_spot = (target % N_PCOL * CB_DEV + target // N_PCOL).astype(jnp.int32)
    split_row = factor_rows.shape[0]

    def stacked_block(spot):
        start = (spot * PB).astype(jnp.int32)
        upper_part = lax.dynamic_slice_in_dim(factor_rows, start, PB, 1)
        lower_part = lax.dynamic_slice_in_dim(measurements, start, PB, 1)
        keep_block = lax.dynamic_slice_in_dim(keep_rows, spot.astype(jnp.int32), 1, 1)
        lower_part = jnp.where(keep_block, lower_part, jnp.zeros_like(lower_part))
        return jnp.concatenate([upper_part, lower_part], axis=0)
    panel_cols = stacked_block(panel_spot)
    gram_matrix = jnp.dot(panel_cols.T, panel_cols, precision=highest)
    lower_factor = cholesky_lower(gram_matrix)
    upper_factor = lower_factor.T
    inverse_lower = invert_lower(lower_factor)

    def update(spot, carry):
        factor_out, measure_out, row_out = carry
        column_block = stacked_block(spot)
        cross_sum = jnp.dot(panel_cols.T, column_block, precision=highest)
        row_share = jnp.dot(inverse_lower, cross_sum, precision=highest)
        row_share = jnp.where(blocks[spot] > target, row_share, jnp.zeros_like(row_share))
        coefficients = jnp.dot(inverse_lower.T, row_share, precision=highest)
        column_block = column_block - jnp.dot(panel_cols, coefficients, precision=highest)
        row_block = row_share + jnp.where(spot == panel_spot, upper_factor, jnp.zeros_like(upper_factor))
        start = (spot * PB).astype(jnp.int32)
        factor_out = lax.dynamic_update_slice_in_dim(factor_out, column_block[:split_row], start, 1)
        measure_out = lax.dynamic_update_slice_in_dim(measure_out, column_block[split_row:], start, 1)
        row_out = lax.dynamic_update_slice_in_dim(row_out, row_block, start, 1)
        return (factor_out, measure_out, row_out)
    row_start = jnp.zeros((PB, block_count * PB), factor_rows.dtype)
    reduced_factor, reduced_measurements, panel_row = lax.fori_loop(jnp.int32(0), jnp.int32(block_count), update, (factor_rows, measurements, row_start))
    return (reduced_factor, reduced_measurements, panel_row)
```

```python
import functools
import jax, jax.numpy as jnp
from jax import lax
from jax.experimental import pallas as pl
from jax.experimental.pallas import tpu as pltpu
from jax.sharding import PartitionSpec as P

PB = 256
CB_DEV = 4
GRID_ROWS = 4
CHUNKS = 16

highest = lax.Precision.HIGHEST
high = lax.Precision.HIGH


def spread_kernel(owner, count, own_ref, panel_ref, send_sem, recv_sem):
    rows, cols = GRID_ROWS, count // GRID_ROWS
    home_r, home_c = owner // cols, owner % cols
    back_r = home_r - 1 if home_r > 0 else 1
    back_c = home_c - 1 if home_c > 0 else 1
    size = own_ref.shape[0] // (2 * CHUNKS)
    me = lax.axis_index("pcol")
    r, c = me // cols, me % cols
    same_r, same_c = r == home_r, c == home_c
    off_r, off_c = r != home_r, c != home_c
    links = (
        (r < rows - 1, cols), (r > 0, -cols), (c < cols - 1, 1), (c > 0, -1),
    )
    away = (r >= home_r, r <= home_r, c >= home_c, c <= home_c)
    fill = (
        off_c & (r == back_r) & (back_r < home_r), off_c & (r == back_r) & (back_r > home_r),
        off_r & (c == back_c) & (back_c < home_c), off_r & (c == back_c) & (back_c > home_c),
    )
    sends = (
        [links[0][0] & ((same_c & away[0]) | fill[0]), links[1][0] & ((same_c & away[1]) | fill[1]),
         links[2][0] & off_r & away[2], links[3][0] & off_r & away[3]],
        [links[0][0] & off_c & away[0], links[1][0] & off_c & away[1],
         links[2][0] & ((same_r & away[2]) | fill[2]), links[3][0] & ((same_r & away[3]) | fill[3])],
    )
    far_r, far_c = jnp.abs(r - home_r), jnp.abs(c - home_c)
    depths = (
        jnp.where(same_r & off_c, far_c + 2, far_r + far_c),
        jnp.where(same_c & off_r, far_r + 2, far_r + far_c),
    )
    mine = same_r & same_c

    @pl.when(mine)
    def _():
        panel_ref[...] = own_ref[...]

    barrier = pltpu.get_barrier_semaphore()
    for there, step in links:
        @pl.when(there)
        def _():
            pl.semaphore_signal(
                barrier, inc=1, device_id={"pcol": me + step}, device_id_type=pl.DeviceIdType.MESH
            )
    pl.semaphore_wait(barrier, sum(there.astype(jnp.int32) for there, _ in links))

    def copy(half, way, chunk):
        start = pl.multiple_of((half * CHUNKS + chunk) * size, size)
        block = panel_ref.at[pl.ds(start, size)]
        return pltpu.make_async_remote_copy(
            src_ref=block,
            dst_ref=block,
            send_sem=send_sem.at[half, way, chunk],
            recv_sem=recv_sem.at[half, chunk],
            device_id={"pcol": me + links[way][1]},
            device_id_type=pl.DeviceIdType.MESH,
        )

    def step(t, carry):
        for half in range(2):
            chunk = t - depths[half]

            @pl.when((chunk >= 0) & (chunk < CHUNKS))
            def _():
                @pl.when(jnp.logical_not(mine))
                def _():
                    copy(half, 0, chunk).wait_recv()

                for way in range(4):
                    @pl.when(sends[half][way])
                    def _():
                        copy(half, way, chunk).start()
        return carry

    lax.fori_loop(0, CHUNKS + rows + cols, step, 0)

    def finish(chunk, carry):
        for half in range(2):
            for way in range(4):
                @pl.when(sends[half][way])
                def _():
                    copy(half, way, chunk).wait_send()
        return carry

    lax.fori_loop(0, CHUNKS, finish, 0)


def spread(own, owner, count):
    def from_owner(index):
        return pl.pallas_call(
            functools.partial(spread_kernel, index, count),
            out_shape=jax.ShapeDtypeStruct(own.shape, own.dtype),
            in_specs=[pl.BlockSpec(memory_space=pltpu.VMEM)],
            out_specs=pl.BlockSpec(memory_space=pltpu.VMEM),
            scratch_shapes=[
                pltpu.SemaphoreType.DMA((2, 4, CHUNKS)),
                pltpu.SemaphoreType.DMA((2, CHUNKS)),
            ],
            compiler_params=pltpu.CompilerParams(
                collective_id=index, has_side_effects=True, vmem_limit_bytes=16 << 20
            ),
        )

    return lax.switch(owner, [from_owner(index) for index in range(count)], own)


def eliminate(square, width, group):
    identity = (
        lax.broadcasted_iota(jnp.int32, (width, width), 0)
        == lax.broadcasted_iota(jnp.int32, (width, width), 1)
    ).astype(jnp.float32)
    strips = [jnp.concatenate([square[k:k + 8], identity[k:k + 8]], axis=1) for k in range(0, width, 8)]
    lanes = 2 * width
    for start in range(0, width, group):
        first = start // 8
        columns = []
        for j in range(start, start + group):
            columns.append([jnp.broadcast_to(strips[s][:, j:j + 1], (8, lanes)) for s in range(first, len(strips))])
        for k in range(group):
            j = start + k
            own, row = j // 8 - first, j % 8
            inverse = 1.0 / columns[k][own][row:row + 1]
            pivot_row = strips[j // 8][row:row + 1] * inverse
            below = lax.broadcasted_iota(jnp.int32, (8, lanes), 0) > row
            factors = [columns[k][s] if s > own else jnp.where(below, columns[k][s], 0.0) for s in range(own, len(columns[k]))]
            for l in range(k + 1, group):
                scale = columns[l][own][row:row + 1] * inverse
                for s in range(own, len(columns[l])):
                    columns[l][s] = columns[l][s] - factors[s - own] * scale
            for s in range(own, len(columns[k])):
                strips[first + s] = strips[first + s] - factors[s - own] * pivot_row
    whole = jnp.concatenate(strips, axis=0)
    pivots = jnp.sum(whole[:, :width] * identity, axis=1, keepdims=True)
    whole = whole * (1.0 / jnp.sqrt(pivots))
    return whole[:, width:]

def factor_kernel(width, group, gram_ref, upper_ref, inverse_ref, work):
    order = gram_ref.shape[0]
    work[...] = gram_ref[...]
    column = lax.broadcasted_iota(jnp.int32, (width, order), 1)
    for start in range(0, order, width):
        stop = start + width
        block_inverse = eliminate(work[start:stop, start:stop], width, group)
        rows = jnp.dot(block_inverse, work[start:stop, :], precision=highest, preferred_element_type=jnp.float32)
        upper = jnp.where(column >= start + lax.broadcasted_iota(jnp.int32, (width, order), 0), rows, 0.0)
        upper_ref[start:stop, :] = upper
        pad = [jnp.zeros((width, start), jnp.float32)] * (start > 0) + [block_inverse]
        pad += [jnp.zeros((width, order - stop), jnp.float32)] * (stop < order)
        placed = jnp.concatenate(pad, axis=1) if len(pad) > 1 else pad[0]
        inverse = jnp.where(column < start, rows, placed)
        inverse_ref[start:stop, :] = inverse
        if stop < order:
            inside = (column >= start) & (column < stop)
            rows = jnp.where(inside, placed, rows)
            rest = work[stop:, :]
            rest_column = lax.broadcasted_iota(jnp.int32, rest.shape, 1)
            rest = jnp.where((rest_column >= start) & (rest_column < stop), 0.0, rest)
            taken = lax.dot_general(upper, rows, (((0,), (0,)), ((), ())), precision=highest, preferred_element_type=jnp.float32)
            work[stop:, :] = rest - taken[stop:, :]

def factor(gram, width=64, group=8):
    order = gram.shape[0]
    shape = jax.ShapeDtypeStruct((order, order), jnp.float32)
    return pl.pallas_call(
        functools.partial(factor_kernel, width, group),
        out_shape=(shape, shape),
        in_specs=[pl.BlockSpec(memory_space=pltpu.VMEM)],
        out_specs=[pl.BlockSpec(memory_space=pltpu.VMEM)] * 2,
        scratch_shapes=[pltpu.VMEM((order, order), jnp.float32)],
        compiler_params=pltpu.CompilerParams(vmem_limit_bytes=32 << 20),
        cost_estimate=pl.CostEstimate(flops=2000000000, bytes_accessed=800000, transcendentals=0),
    )(gram)


def exchange_sum(partial, axis):
    count = lax.axis_size(axis)
    distance = 1
    while distance < count:
        pairs = [(i, i ^ distance) for i in range(count)]
        partial = partial + lax.ppermute(partial, axis, pairs)
        distance *= 2
    return partial


def products(left, right, precision):
    return lax.dot_general(left, right, (((0,), (0,)), ((), ())), precision=precision)


def local(factor_rows, measurements, link_blocks, panel_index):
    column = lax.axis_index("pcol")
    count = lax.axis_size("pcol")
    blocks = jnp.arange(CB_DEV, dtype=jnp.int32) * count + column
    touched = jnp.any(link_blocks[:, :, None] == blocks[None, None, :], axis=1)
    shaped = measurements.reshape(touched.shape[0], PB, CB_DEV, PB)
    masked = jnp.where(touched[:, None, :, None], shaped, 0.0).reshape(measurements.shape)
    split_row = factor_rows.shape[0]
    target = panel_index[0]
    slot, owner = target // count, target % count
    own = jnp.concatenate([
        lax.dynamic_slice_in_dim(factor_rows, slot * PB, PB, 1),
        lax.dynamic_slice_in_dim(masked, slot * PB, PB, 1),
    ], axis=0)
    later = jnp.repeat(blocks > target, PB)[None, :]
    at_panel = jnp.repeat(blocks == target, PB)[None, :]
    panel = spread(own, owner, count)
    panel_f, panel_m = panel[:split_row], panel[split_row:]
    gram = exchange_sum(products(panel, panel, highest), "prow")
    upper, inverse_lower = factor(gram)
    cross = products(panel_f, factor_rows, high) + products(panel_m, masked, high)
    cross = exchange_sum(cross, "prow")
    share = jnp.where(later, jnp.dot(inverse_lower, cross, precision=highest), 0.0)
    coefficients = products(inverse_lower, share, highest)
    reduced_f = factor_rows - jnp.dot(panel_f, coefficients, precision=high)
    reduced_m = masked - jnp.dot(panel_m, coefficients, precision=high)
    panel_row = share + jnp.where(at_panel, jnp.tile(upper, (1, CB_DEV)), 0.0)
    return (reduced_f, reduced_m, panel_row)


def solution(mesh):
    in_specs = (P("prow", "pcol"), P("prow", "pcol"), P("prow", None), P())
    out_specs = (P("prow", "pcol"), P("prow", "pcol"), P(None, "pcol"))
    return jax.shard_map(local, mesh=mesh, in_specs=in_specs, out_specs=out_specs, check_vma=False)
```

```python
import functools
import jax, jax.numpy as jnp
from jax import lax
from jax.experimental import pallas as pl
from jax.experimental.pallas import tpu as pltpu
from jax.sharding import PartitionSpec as P

PB = 256
CB_DEV = 4
GRID_ROWS = 4
CHUNKS = 16
SKEW = 4

highest = lax.Precision.HIGHEST
high = lax.Precision.HIGH


def spread_kernel(owner, count, own_ref, panel_ref, send_sem, recv_sem):
    rows, cols = GRID_ROWS, count // GRID_ROWS
    home_r, home_c = owner // cols, owner % cols
    back_r = home_r - 1 if home_r > 0 else 1
    back_c = home_c - 1 if home_c > 0 else 1
    size = own_ref.shape[0] // (2 * CHUNKS)
    me = lax.axis_index("pcol")
    r, c = me // cols, me % cols
    same_r, same_c = r == home_r, c == home_c
    off_r, off_c = r != home_r, c != home_c
    links = (
        (r < rows - 1, cols), (r > 0, -cols), (c < cols - 1, 1), (c > 0, -1),
    )
    away = (r >= home_r, r <= home_r, c >= home_c, c <= home_c)
    fill = (
        off_c & (r == back_r) & (back_r < home_r), off_c & (r == back_r) & (back_r > home_r),
        off_r & (c == back_c) & (back_c < home_c), off_r & (c == back_c) & (back_c > home_c),
    )
    sends = (
        [links[0][0] & ((same_c & away[0]) | fill[0]), links[1][0] & ((same_c & away[1]) | fill[1]),
         links[2][0] & off_r & away[2], links[3][0] & off_r & away[3]],
        [links[0][0] & off_c & away[0], links[1][0] & off_c & away[1],
         links[2][0] & ((same_r & away[2]) | fill[2]), links[3][0] & ((same_r & away[3]) | fill[3])],
    )
    far_r, far_c = jnp.abs(r - home_r), jnp.abs(c - home_c)
    depths = (
        jnp.where(same_r & off_c, far_c + 2, far_r + far_c),
        jnp.where(same_c & off_r, far_r + 2, far_r + far_c),
    )
    mine = same_r & same_c

    @pl.when(mine)
    def _():
        panel_ref[...] = own_ref[...]

    barrier = pltpu.get_barrier_semaphore()
    for there, step in links:
        @pl.when(there)
        def _():
            pl.semaphore_signal(
                barrier, inc=1, device_id={"pcol": me + step}, device_id_type=pl.DeviceIdType.MESH
            )
    pl.semaphore_wait(barrier, sum(there.astype(jnp.int32) for there, _ in links))

    def copy(half, way, chunk):
        start = pl.multiple_of((half * CHUNKS + chunk) * size, size)
        block = panel_ref.at[pl.ds(start, size)]
        return pltpu.make_async_remote_copy(
            src_ref=block,
            dst_ref=block,
            send_sem=send_sem.at[half, way, chunk],
            recv_sem=recv_sem.at[half, chunk],
            device_id={"pcol": me + links[way][1]},
            device_id_type=pl.DeviceIdType.MESH,
        )

    def step(t, carry):
        for half in range(2):
            chunk = t - SKEW * depths[half]

            @pl.when((chunk >= 0) & (chunk < CHUNKS))
            def _():
                @pl.when(jnp.logical_not(mine))
                def _():
                    copy(half, 0, chunk).wait_recv()

                for way in range(4):
                    @pl.when(sends[half][way])
                    def _():
                        copy(half, way, chunk).start()
        return carry

    lax.fori_loop(0, CHUNKS + SKEW * (rows + cols), step, 0)

    def finish(chunk, carry):
        for half in range(2):
            for way in range(4):
                @pl.when(sends[half][way])
                def _():
                    copy(half, way, chunk).wait_send()
        return carry

    lax.fori_loop(0, CHUNKS, finish, 0)


def spread(own, owner, count):
    def from_owner(index):
        return pl.pallas_call(
            functools.partial(spread_kernel, index, count),
            out_shape=jax.ShapeDtypeStruct(own.shape, own.dtype),
            in_specs=[pl.BlockSpec(memory_space=pltpu.VMEM)],
            out_specs=pl.BlockSpec(memory_space=pltpu.VMEM),
            scratch_shapes=[
                pltpu.SemaphoreType.DMA((2, 4, CHUNKS)),
                pltpu.SemaphoreType.DMA((2, CHUNKS)),
            ],
            compiler_params=pltpu.CompilerParams(
                collective_id=index, has_side_effects=True, vmem_limit_bytes=16 << 20
            ),
        )

    return lax.switch(owner, [from_owner(index) for index in range(count)], own)


def eliminate(square, width, group):
    identity = (
        lax.broadcasted_iota(jnp.int32, (width, width), 0)
        == lax.broadcasted_iota(jnp.int32, (width, width), 1)
    ).astype(jnp.float32)
    strips = [jnp.concatenate([square[k:k + 8], identity[k:k + 8]], axis=1) for k in range(0, width, 8)]
    lanes = 2 * width
    for start in range(0, width, group):
        first = start // 8
        columns = []
        for j in range(start, start + group):
            columns.append([jnp.broadcast_to(strips[s][:, j:j + 1], (8, lanes)) for s in range(first, len(strips))])
        for k in range(group):
            j = start + k
            own, row = j // 8 - first, j % 8
            inverse = 1.0 / columns[k][own][row:row + 1]
            pivot_row = strips[j // 8][row:row + 1] * inverse
            below = lax.broadcasted_iota(jnp.int32, (8, lanes), 0) > row
            factors = [columns[k][s] if s > own else jnp.where(below, columns[k][s], 0.0) for s in range(own, len(columns[k]))]
            for l in range(k + 1, group):
                scale = columns[l][own][row:row + 1] * inverse
                for s in range(own, len(columns[l])):
                    columns[l][s] = columns[l][s] - factors[s - own] * scale
            for s in range(own, len(columns[k])):
                strips[first + s] = strips[first + s] - factors[s - own] * pivot_row
    whole = jnp.concatenate(strips, axis=0)
    pivots = jnp.sum(whole[:, :width] * identity, axis=1, keepdims=True)
    whole = whole * (1.0 / jnp.sqrt(pivots))
    return whole[:, width:]

def factor_kernel(width, group, gram_ref, upper_ref, inverse_ref, work):
    order = gram_ref.shape[0]
    work[...] = gram_ref[...]
    column = lax.broadcasted_iota(jnp.int32, (width, order), 1)
    for start in range(0, order, width):
        stop = start + width
        block_inverse = eliminate(work[start:stop, start:stop], width, group)
        rows = jnp.dot(block_inverse, work[start:stop, :], precision=highest, preferred_element_type=jnp.float32)
        upper = jnp.where(column >= start + lax.broadcasted_iota(jnp.int32, (width, order), 0), rows, 0.0)
        upper_ref[start:stop, :] = upper
        pad = [jnp.zeros((width, start), jnp.float32)] * (start > 0) + [block_inverse]
        pad += [jnp.zeros((width, order - stop), jnp.float32)] * (stop < order)
        placed = jnp.concatenate(pad, axis=1) if len(pad) > 1 else pad[0]
        inverse = jnp.where(column < start, rows, placed)
        inverse_ref[start:stop, :] = inverse
        if stop < order:
            inside = (column >= start) & (column < stop)
            rows = jnp.where(inside, placed, rows)
            rest = work[stop:, :]
            rest_column = lax.broadcasted_iota(jnp.int32, rest.shape, 1)
            rest = jnp.where((rest_column >= start) & (rest_column < stop), 0.0, rest)
            taken = lax.dot_general(upper, rows, (((0,), (0,)), ((), ())), precision=highest, preferred_element_type=jnp.float32)
            work[stop:, :] = rest - taken[stop:, :]

def factor(gram, width=64, group=8):
    order = gram.shape[0]
    shape = jax.ShapeDtypeStruct((order, order), jnp.float32)
    return pl.pallas_call(
        functools.partial(factor_kernel, width, group),
        out_shape=(shape, shape),
        in_specs=[pl.BlockSpec(memory_space=pltpu.VMEM)],
        out_specs=[pl.BlockSpec(memory_space=pltpu.VMEM)] * 2,
        scratch_shapes=[pltpu.VMEM((order, order), jnp.float32)],
        compiler_params=pltpu.CompilerParams(vmem_limit_bytes=32 << 20),
        cost_estimate=pl.CostEstimate(flops=2000000000, bytes_accessed=800000, transcendentals=0),
    )(gram)


def swap(block, axis, distance):
    count = lax.axis_size(axis)
    return lax.ppermute(block, axis, [(i, i ^ distance) for i in range(count)])


def halve(partial, axis):
    half = partial.shape[0] // 2
    core = lax.axis_index(axis) % 2
    kept = lax.dynamic_slice_in_dim(partial, core * half, half, 0)
    given = lax.dynamic_slice_in_dim(partial, (1 - core) * half, half, 0)
    return kept + swap(given, axis, 1)


def across(half, axis):
    distance = 2
    while distance < lax.axis_size(axis):
        half = half + swap(half, axis, distance)
        distance *= 2
    return half


def rejoin(half, axis):
    other = swap(half, axis, 1)
    even = lax.axis_index(axis) % 2 == 0
    return jnp.concatenate([jnp.where(even, half, other), jnp.where(even, other, half)], axis=0)


def products(left, right, precision):
    return lax.dot_general(left, right, (((0,), (0,)), ((), ())), precision=precision)


def local(factor_rows, measurements, link_blocks, panel_index):
    column = lax.axis_index("pcol")
    count = lax.axis_size("pcol")
    blocks = jnp.arange(CB_DEV, dtype=jnp.int32) * count + column
    touched = jnp.any(link_blocks[:, :, None] == blocks[None, None, :], axis=1)
    shaped = measurements.reshape(touched.shape[0], PB, CB_DEV, PB)
    masked = jnp.where(touched[:, None, :, None], shaped, 0.0).reshape(measurements.shape)
    split_row = factor_rows.shape[0]
    target = panel_index[0]
    slot, owner = target // count, target % count
    own = jnp.concatenate([
        lax.dynamic_slice_in_dim(factor_rows, slot * PB, PB, 1),
        lax.dynamic_slice_in_dim(masked, slot * PB, PB, 1),
    ], axis=0)
    later = jnp.repeat(blocks > target, PB)[None, :]
    at_panel = jnp.repeat(blocks == target, PB)[None, :]
    panel = spread(own, owner, count)
    panel_f, panel_m = panel[:split_row], panel[split_row:]
    gram = halve(products(panel, panel, highest), "prow")
    gram = rejoin(across(gram, "prow"), "prow")
    cross = products(panel_f, factor_rows, high) + products(panel_m, masked, high)
    cross = halve(cross, "prow")
    gram, cross = lax.optimization_barrier((gram, cross))
    upper, inverse_lower = factor(gram)
    cross = rejoin(across(cross, "prow"), "prow")
    share = jnp.where(later, jnp.dot(inverse_lower, cross, precision=highest), 0.0)
    coefficients = products(inverse_lower, share, highest)
    reduced_f = factor_rows - jnp.dot(panel_f, coefficients, precision=high)
    reduced_m = masked - jnp.dot(panel_m, coefficients, precision=high)
    panel_row = share + jnp.where(at_panel, jnp.tile(upper, (1, CB_DEV)), 0.0)
    return (reduced_f, reduced_m, panel_row)


def solution(mesh):
    in_specs = (P("prow", "pcol"), P("prow", "pcol"), P("prow", None), P())
    out_specs = (P("prow", "pcol"), P("prow", "pcol"), P(None, "pcol"))
    return jax.shard_map(local, mesh=mesh, in_specs=in_specs, out_specs=out_specs, check_vma=False)
```

```python
import functools
import jax, jax.numpy as jnp
from jax import lax
from jax.experimental import pallas as pl
from jax.experimental.pallas import tpu as pltpu
from jax.sharding import PartitionSpec as P

PB = 256
CB_DEV = 4
GRID_ROWS = 4
CHUNKS = 16
SKEW = 4

highest = lax.Precision.HIGHEST
high = lax.Precision.HIGH


def spread_kernel(owner, count, own_ref, panel_ref, send_sem, recv_sem):
    rows, cols = GRID_ROWS, count // GRID_ROWS
    home_r, home_c = owner // cols, owner % cols
    back_r = home_r - 1 if home_r > 0 else 1
    back_c = home_c - 1 if home_c > 0 else 1
    size = own_ref.shape[0] // (2 * CHUNKS)
    me = lax.axis_index("pcol")
    r, c = me // cols, me % cols
    same_r, same_c = r == home_r, c == home_c
    off_r, off_c = r != home_r, c != home_c
    links = (
        (r < rows - 1, cols), (r > 0, -cols), (c < cols - 1, 1), (c > 0, -1),
    )
    away = (r >= home_r, r <= home_r, c >= home_c, c <= home_c)
    fill = (
        off_c & (r == back_r) & (back_r < home_r), off_c & (r == back_r) & (back_r > home_r),
        off_r & (c == back_c) & (back_c < home_c), off_r & (c == back_c) & (back_c > home_c),
    )
    sends = (
        [links[0][0] & ((same_c & away[0]) | fill[0]), links[1][0] & ((same_c & away[1]) | fill[1]),
         links[2][0] & off_r & away[2], links[3][0] & off_r & away[3]],
        [links[0][0] & off_c & away[0], links[1][0] & off_c & away[1],
         links[2][0] & ((same_r & away[2]) | fill[2]), links[3][0] & ((same_r & away[3]) | fill[3])],
    )
    far_r, far_c = jnp.abs(r - home_r), jnp.abs(c - home_c)
    depths = (
        jnp.where(same_r & off_c, far_c + 2, far_r + far_c),
        jnp.where(same_c & off_r, far_r + 2, far_r + far_c),
    )
    mine = same_r & same_c

    @pl.when(mine)
    def _():
        panel_ref[...] = own_ref[...]

    barrier = pltpu.get_barrier_semaphore()
    for there, step in links:
        @pl.when(there)
        def _():
            pl.semaphore_signal(
                barrier, inc=1, device_id={"pcol": me + step}, device_id_type=pl.DeviceIdType.MESH
            )
    pl.semaphore_wait(barrier, sum(there.astype(jnp.int32) for there, _ in links))

    def copy(half, way, chunk):
        start = pl.multiple_of((half * CHUNKS + chunk) * size, size)
        block = panel_ref.at[pl.ds(start, size)]
        return pltpu.make_async_remote_copy(
            src_ref=block,
            dst_ref=block,
            send_sem=send_sem.at[half, way, chunk],
            recv_sem=recv_sem.at[half, chunk],
            device_id={"pcol": me + links[way][1]},
            device_id_type=pl.DeviceIdType.MESH,
        )

    def step(t, carry):
        for half in range(2):
            chunk = t - SKEW * depths[half]

            @pl.when((chunk >= 0) & (chunk < CHUNKS))
            def _():
                @pl.when(jnp.logical_not(mine))
                def _():
                    copy(half, 0, chunk).wait_recv()

                for way in range(4):
                    @pl.when(sends[half][way])
                    def _():
                        copy(half, way, chunk).start()
        return carry

    lax.fori_loop(0, CHUNKS + SKEW * (rows + cols), step, 0)

    def finish(chunk, carry):
        for half in range(2):
            for way in range(4):
                @pl.when(sends[half][way])
                def _():
                    copy(half, way, chunk).wait_send()
        return carry

    lax.fori_loop(0, CHUNKS, finish, 0)


def spread(own, owner, count):
    def from_owner(index):
        return pl.pallas_call(
            functools.partial(spread_kernel, index, count),
            out_shape=jax.ShapeDtypeStruct(own.shape, own.dtype),
            in_specs=[pl.BlockSpec(memory_space=pltpu.VMEM)],
            out_specs=pl.BlockSpec(memory_space=pltpu.VMEM),
            scratch_shapes=[
                pltpu.SemaphoreType.DMA((2, 4, CHUNKS)),
                pltpu.SemaphoreType.DMA((2, CHUNKS)),
            ],
            compiler_params=pltpu.CompilerParams(
                collective_id=index, has_side_effects=True, vmem_limit_bytes=16 << 20
            ),
        )

    return lax.switch(owner, [from_owner(index) for index in range(count)], own)


def eliminate(square, width, group):
    identity = (
        lax.broadcasted_iota(jnp.int32, (width, width), 0)
        == lax.broadcasted_iota(jnp.int32, (width, width), 1)
    ).astype(jnp.float32)
    strips = [jnp.concatenate([square[k:k + 8], identity[k:k + 8]], axis=1) for k in range(0, width, 8)]
    lanes = 2 * width
    for start in range(0, width, group):
        first = start // 8
        columns = []
        for j in range(start, start + group):
            columns.append([jnp.broadcast_to(strips[s][:, j:j + 1], (8, lanes)) for s in range(first, len(strips))])
        for k in range(group):
            j = start + k
            own, row = j // 8 - first, j % 8
            inverse = 1.0 / columns[k][own][row:row + 1]
            pivot_row = strips[j // 8][row:row + 1] * inverse
            below = lax.broadcasted_iota(jnp.int32, (8, lanes), 0) > row
            factors = [columns[k][s] if s > own else jnp.where(below, columns[k][s], 0.0) for s in range(own, len(columns[k]))]
            for l in range(k + 1, group):
                scale = columns[l][own][row:row + 1] * inverse
                for s in range(own, len(columns[l])):
                    columns[l][s] = columns[l][s] - factors[s - own] * scale
            for s in range(own, len(columns[k])):
                strips[first + s] = strips[first + s] - factors[s - own] * pivot_row
    whole = jnp.concatenate(strips, axis=0)
    pivots = jnp.sum(whole[:, :width] * identity, axis=1, keepdims=True)
    whole = whole * (1.0 / jnp.sqrt(pivots))
    return whole[:, width:]

def factor_kernel(width, group, gram_ref, upper_ref, inverse_ref, work):
    order = gram_ref.shape[0]
    work[...] = gram_ref[...]
    column = lax.broadcasted_iota(jnp.int32, (width, order), 1)
    for start in range(0, order, width):
        stop = start + width
        block_inverse = eliminate(work[start:stop, start:stop], width, group)
        rows = jnp.dot(block_inverse, work[start:stop, :], precision=highest, preferred_element_type=jnp.float32)
        upper = jnp.where(column >= start + lax.broadcasted_iota(jnp.int32, (width, order), 0), rows, 0.0)
        upper_ref[start:stop, :] = upper
        pad = [jnp.zeros((width, start), jnp.float32)] * (start > 0) + [block_inverse]
        pad += [jnp.zeros((width, order - stop), jnp.float32)] * (stop < order)
        placed = jnp.concatenate(pad, axis=1) if len(pad) > 1 else pad[0]
        inverse = jnp.where(column < start, rows, placed)
        inverse_ref[start:stop, :] = inverse
        if stop < order:
            inside = (column >= start) & (column < stop)
            rows = jnp.where(inside, placed, rows)
            rest = work[stop:, :]
            rest_column = lax.broadcasted_iota(jnp.int32, rest.shape, 1)
            rest = jnp.where((rest_column >= start) & (rest_column < stop), 0.0, rest)
            taken = lax.dot_general(upper, rows, (((0,), (0,)), ((), ())), precision=highest, preferred_element_type=jnp.float32)
            work[stop:, :] = rest - taken[stop:, :]

def factor(gram, width=64, group=8):
    order = gram.shape[0]
    shape = jax.ShapeDtypeStruct((order, order), jnp.float32)
    return pl.pallas_call(
        functools.partial(factor_kernel, width, group),
        out_shape=(shape, shape),
        in_specs=[pl.BlockSpec(memory_space=pltpu.VMEM)],
        out_specs=[pl.BlockSpec(memory_space=pltpu.VMEM)] * 2,
        scratch_shapes=[pltpu.VMEM((order, order), jnp.float32)],
        compiler_params=pltpu.CompilerParams(vmem_limit_bytes=32 << 20),
        cost_estimate=pl.CostEstimate(flops=2000000000, bytes_accessed=800000, transcendentals=0),
    )(gram)


def swap(block, axis, distance):
    count = lax.axis_size(axis)
    return lax.ppermute(block, axis, [(i, i ^ distance) for i in range(count)])


def halve(partial, axis):
    half = partial.shape[0] // 2
    core = lax.axis_index(axis) % 2
    kept = lax.dynamic_slice_in_dim(partial, core * half, half, 0)
    given = lax.dynamic_slice_in_dim(partial, (1 - core) * half, half, 0)
    return kept + swap(given, axis, 1)


def across(half, axis):
    distance = 2
    while distance < lax.axis_size(axis):
        half = half + swap(half, axis, distance)
        distance *= 2
    return half


def rejoin(half, axis):
    other = swap(half, axis, 1)
    even = lax.axis_index(axis) % 2 == 0
    return jnp.concatenate([jnp.where(even, half, other), jnp.where(even, other, half)], axis=0)


def products(left, right, precision):
    return lax.dot_general(left, right, (((0,), (0,)), ((), ())), precision=precision)


def local(factor_rows, measurements, link_blocks, panel_index):
    column = lax.axis_index("pcol")
    count = lax.axis_size("pcol")
    blocks = jnp.arange(CB_DEV, dtype=jnp.int32) * count + column
    split_row = factor_rows.shape[0]
    target = panel_index[0]
    slot, owner = target // count, target % count
    own_touched = jnp.any(link_blocks == slot * count + column, axis=1)
    own_rows = lax.dynamic_slice_in_dim(measurements, slot * PB, PB, 1)
    own = jnp.concatenate([
        lax.dynamic_slice_in_dim(factor_rows, slot * PB, PB, 1),
        jnp.where(jnp.repeat(own_touched, PB)[:, None], own_rows, 0.0),
    ], axis=0)
    later = jnp.repeat(blocks > target, PB)[None, :]
    at_panel = jnp.repeat(blocks == target, PB)[None, :]
    panel = spread(own, owner, count)
    panel, link_blocks = lax.optimization_barrier((panel, link_blocks))
    touched = jnp.any(link_blocks[:, :, None] == blocks[None, None, :], axis=1)
    shaped = measurements.reshape(touched.shape[0], PB, CB_DEV, PB)
    masked = jnp.where(touched[:, None, :, None], shaped, 0.0).reshape(measurements.shape)
    panel_f, panel_m = panel[:split_row], panel[split_row:]
    gram = halve(products(panel, panel, highest), "prow")
    gram = rejoin(across(gram, "prow"), "prow")
    cross = products(panel_f, factor_rows, high) + products(panel_m, masked, high)
    cross = halve(cross, "prow")
    gram, cross = lax.optimization_barrier((gram, cross))
    upper, inverse_lower = factor(gram)
    cross = across(cross, "prow")
    upper, inverse_lower, cross = lax.optimization_barrier((upper, inverse_lower, cross))
    cross = rejoin(cross, "prow")
    share = jnp.where(later, jnp.dot(inverse_lower, cross, precision=highest), 0.0)
    coefficients = products(inverse_lower, share, highest)
    reduced_f = factor_rows - jnp.dot(panel_f, coefficients, precision=high)
    reduced_m = masked - jnp.dot(panel_m, coefficients, precision=high)
    panel_row = share + jnp.where(at_panel, jnp.tile(upper, (1, CB_DEV)), 0.0)
    return (reduced_f, reduced_m, panel_row)


def solution(mesh):
    in_specs = (P("prow", "pcol"), P("prow", "pcol"), P("prow", None), P())
    out_specs = (P("prow", "pcol"), P("prow", "pcol"), P(None, "pcol"))
    return jax.shard_map(local, mesh=mesh, in_specs=in_specs, out_specs=out_specs, check_vma=False)
```

```python
import functools
import jax, jax.numpy as jnp
from jax import lax
from jax.experimental import pallas as pl
from jax.experimental.pallas import tpu as pltpu
from jax.sharding import PartitionSpec as P

PB = 256
CB_DEV = 4
GRID_ROWS = 4
CHUNKS = 16
SKEW = 4

highest = lax.Precision.HIGHEST
high = lax.Precision.HIGH


def spread_kernel(owner, count, own_ref, panel_ref, send_sem, recv_sem):
    rows, cols = GRID_ROWS, count // GRID_ROWS
    home_r, home_c = owner // cols, owner % cols
    back_r = home_r - 1 if home_r > 0 else 1
    back_c = home_c - 1 if home_c > 0 else 1
    size = own_ref.shape[0] // (2 * CHUNKS)
    me = lax.axis_index("pcol")
    r, c = me // cols, me % cols
    same_r, same_c = r == home_r, c == home_c
    off_r, off_c = r != home_r, c != home_c
    links = (
        (r < rows - 1, cols), (r > 0, -cols), (c < cols - 1, 1), (c > 0, -1),
    )
    away = (r >= home_r, r <= home_r, c >= home_c, c <= home_c)
    fill = (
        off_c & (r == back_r) & (back_r < home_r), off_c & (r == back_r) & (back_r > home_r),
        off_r & (c == back_c) & (back_c < home_c), off_r & (c == back_c) & (back_c > home_c),
    )
    sends = (
        [links[0][0] & ((same_c & away[0]) | fill[0]), links[1][0] & ((same_c & away[1]) | fill[1]),
         links[2][0] & off_r & away[2], links[3][0] & off_r & away[3]],
        [links[0][0] & off_c & away[0], links[1][0] & off_c & away[1],
         links[2][0] & ((same_r & away[2]) | fill[2]), links[3][0] & ((same_r & away[3]) | fill[3])],
    )
    far_r, far_c = jnp.abs(r - home_r), jnp.abs(c - home_c)
    depths = (
        jnp.where(same_r & off_c, far_c + 2, far_r + far_c),
        jnp.where(same_c & off_r, far_r + 2, far_r + far_c),
    )
    mine = same_r & same_c

    @pl.when(mine)
    def _():
        panel_ref[...] = own_ref[...]

    barrier = pltpu.get_barrier_semaphore()
    for there, step in links:
        @pl.when(there)
        def _():
            pl.semaphore_signal(
                barrier, inc=1, device_id={"pcol": me + step}, device_id_type=pl.DeviceIdType.MESH
            )
    pl.semaphore_wait(barrier, sum(there.astype(jnp.int32) for there, _ in links))

    def copy(half, way, chunk):
        start = pl.multiple_of((half * CHUNKS + chunk) * size, size)
        block = panel_ref.at[pl.ds(start, size)]
        return pltpu.make_async_remote_copy(
            src_ref=block,
            dst_ref=block,
            send_sem=send_sem.at[half, way, chunk],
            recv_sem=recv_sem.at[half, chunk],
            device_id={"pcol": me + links[way][1]},
            device_id_type=pl.DeviceIdType.MESH,
        )

    def step(t, carry):
        for half in range(2):
            chunk = t - SKEW * depths[half]

            @pl.when((chunk >= 0) & (chunk < CHUNKS))
            def _():
                @pl.when(jnp.logical_not(mine))
                def _():
                    copy(half, 0, chunk).wait_recv()

                for way in range(4):
                    @pl.when(sends[half][way])
                    def _():
                        copy(half, way, chunk).start()
        return carry

    lax.fori_loop(0, CHUNKS + SKEW * (rows + cols), step, 0)

    def finish(chunk, carry):
        for half in range(2):
            for way in range(4):
                @pl.when(sends[half][way])
                def _():
                    copy(half, way, chunk).wait_send()
        return carry

    lax.fori_loop(0, CHUNKS, finish, 0)


def spread(own, owner, count):
    def from_owner(index):
        return pl.pallas_call(
            functools.partial(spread_kernel, index, count),
            out_shape=jax.ShapeDtypeStruct(own.shape, own.dtype),
            in_specs=[pl.BlockSpec(memory_space=pltpu.VMEM)],
            out_specs=pl.BlockSpec(memory_space=pltpu.VMEM),
            scratch_shapes=[
                pltpu.SemaphoreType.DMA((2, 4, CHUNKS)),
                pltpu.SemaphoreType.DMA((2, CHUNKS)),
            ],
            compiler_params=pltpu.CompilerParams(
                collective_id=index, has_side_effects=True, vmem_limit_bytes=16 << 20
            ),
        )

    return lax.switch(owner, [from_owner(index) for index in range(count)], own)


def eliminate(square, width, group):
    identity = (
        lax.broadcasted_iota(jnp.int32, (width, width), 0)
        == lax.broadcasted_iota(jnp.int32, (width, width), 1)
    ).astype(jnp.float32)
    strips = [jnp.concatenate([square[k:k + 8], identity[k:k + 8]], axis=1) for k in range(0, width, 8)]
    lanes = 2 * width
    for start in range(0, width, group):
        first = start // 8
        columns = []
        for j in range(start, start + group):
            columns.append([jnp.broadcast_to(strips[s][:, j:j + 1], (8, lanes)) for s in range(first, len(strips))])
        for k in range(group):
            j = start + k
            own, row = j // 8 - first, j % 8
            inverse = 1.0 / columns[k][own][row:row + 1]
            pivot_row = strips[j // 8][row:row + 1] * inverse
            below = lax.broadcasted_iota(jnp.int32, (8, lanes), 0) > row
            factors = [columns[k][s] if s > own else jnp.where(below, columns[k][s], 0.0) for s in range(own, len(columns[k]))]
            for l in range(k + 1, group):
                scale = columns[l][own][row:row + 1] * inverse
                for s in range(own, len(columns[l])):
                    columns[l][s] = columns[l][s] - factors[s - own] * scale
            for s in range(own, len(columns[k])):
                strips[first + s] = strips[first + s] - factors[s - own] * pivot_row
    whole = jnp.concatenate(strips, axis=0)
    pivots = jnp.sum(whole[:, :width] * identity, axis=1, keepdims=True)
    whole = whole * (1.0 / jnp.sqrt(pivots))
    return whole[:, width:]

def factor_kernel(width, group, gram_ref, upper_ref, inverse_ref, work):
    order = gram_ref.shape[0]
    work[...] = gram_ref[...]
    column = lax.broadcasted_iota(jnp.int32, (width, order), 1)
    for start in range(0, order, width):
        stop = start + width
        block_inverse = eliminate(work[start:stop, start:stop], width, group)
        rows = jnp.dot(block_inverse, work[start:stop, :], precision=highest, preferred_element_type=jnp.float32)
        upper = jnp.where(column >= start + lax.broadcasted_iota(jnp.int32, (width, order), 0), rows, 0.0)
        upper_ref[start:stop, :] = upper
        pad = [jnp.zeros((width, start), jnp.float32)] * (start > 0) + [block_inverse]
        pad += [jnp.zeros((width, order - stop), jnp.float32)] * (stop < order)
        placed = jnp.concatenate(pad, axis=1) if len(pad) > 1 else pad[0]
        inverse = jnp.where(column < start, rows, placed)
        inverse_ref[start:stop, :] = inverse
        if stop < order:
            inside = (column >= start) & (column < stop)
            rows = jnp.where(inside, placed, rows)
            rest = work[stop:, :]
            rest_column = lax.broadcasted_iota(jnp.int32, rest.shape, 1)
            rest = jnp.where((rest_column >= start) & (rest_column < stop), 0.0, rest)
            taken = lax.dot_general(upper, rows, (((0,), (0,)), ((), ())), precision=highest, preferred_element_type=jnp.float32)
            work[stop:, :] = rest - taken[stop:, :]

def factor(gram, width=64, group=8):
    order = gram.shape[0]
    shape = jax.ShapeDtypeStruct((order, order), jnp.float32)
    return pl.pallas_call(
        functools.partial(factor_kernel, width, group),
        out_shape=(shape, shape),
        in_specs=[pl.BlockSpec(memory_space=pltpu.VMEM)],
        out_specs=[pl.BlockSpec(memory_space=pltpu.VMEM)] * 2,
        scratch_shapes=[pltpu.VMEM((order, order), jnp.float32)],
        compiler_params=pltpu.CompilerParams(vmem_limit_bytes=32 << 20),
        cost_estimate=pl.CostEstimate(flops=2000000000, bytes_accessed=800000, transcendentals=0),
    )(gram)


def swap(block, axis, distance):
    count = lax.axis_size(axis)
    return lax.ppermute(block, axis, [(i, i ^ distance) for i in range(count)])


def halve(partial, axis):
    half = partial.shape[0] // 2
    core = lax.axis_index(axis) % 2
    kept = lax.dynamic_slice_in_dim(partial, core * half, half, 0)
    given = lax.dynamic_slice_in_dim(partial, (1 - core) * half, half, 0)
    return kept + swap(given, axis, 1)


def across(half, axis):
    distance = 2
    while distance < lax.axis_size(axis):
        half = half + swap(half, axis, distance)
        distance *= 2
    return half


def rejoin(half, axis):
    other = swap(half, axis, 1)
    even = lax.axis_index(axis) % 2 == 0
    return jnp.concatenate([jnp.where(even, half, other), jnp.where(even, other, half)], axis=0)


def products(left, right, precision):
    return lax.dot_general(left, right, (((0,), (0,)), ((), ())), precision=precision)


def local(factor_rows, measurements, link_blocks, panel_index):
    column = lax.axis_index("pcol")
    count = lax.axis_size("pcol")
    blocks = jnp.arange(CB_DEV, dtype=jnp.int32) * count + column
    split_row = factor_rows.shape[0]
    target = panel_index[0]
    slot, owner = target // count, target % count
    own_touched = jnp.any(link_blocks == slot * count + column, axis=1)
    own_rows = lax.dynamic_slice_in_dim(measurements, slot * PB, PB, 1)
    own = jnp.concatenate([
        lax.dynamic_slice_in_dim(factor_rows, slot * PB, PB, 1),
        jnp.where(jnp.repeat(own_touched, PB)[:, None], own_rows, 0.0),
    ], axis=0)
    later = jnp.repeat(blocks > target, PB)[None, :]
    at_panel = jnp.repeat(blocks == target, PB)[None, :]
    panel = spread(own, owner, count)
    gram = halve(products(panel, panel, highest), "prow")
    gram, panel, link_blocks = lax.optimization_barrier((gram, panel, link_blocks))
    touched = jnp.any(link_blocks[:, :, None] == blocks[None, None, :], axis=1)
    shaped = measurements.reshape(touched.shape[0], PB, CB_DEV, PB)
    masked = jnp.where(touched[:, None, :, None], shaped, 0.0).reshape(measurements.shape)
    panel_f, panel_m = panel[:split_row], panel[split_row:]
    gram = across(gram, "prow")
    cross = products(panel_f, factor_rows, high) + products(panel_m, masked, high)
    gram, cross = lax.optimization_barrier((gram, cross))
    cross = halve(cross, "prow")
    upper, inverse_lower = factor(rejoin(gram, "prow"))
    cross = across(cross, "prow")
    upper, inverse_lower, cross = lax.optimization_barrier((upper, inverse_lower, cross))
    cross = rejoin(cross, "prow")
    share = jnp.where(later, jnp.dot(inverse_lower, cross, precision=highest), 0.0)
    coefficients = products(inverse_lower, share, highest)
    reduced_f = factor_rows - jnp.dot(panel_f, coefficients, precision=high)
    reduced_m = masked - jnp.dot(panel_m, coefficients, precision=high)
    panel_row = share + jnp.where(at_panel, jnp.tile(upper, (1, CB_DEV)), 0.0)
    return (reduced_f, reduced_m, panel_row)


def solution(mesh):
    in_specs = (P("prow", "pcol"), P("prow", "pcol"), P("prow", None), P())
    out_specs = (P("prow", "pcol"), P("prow", "pcol"), P(None, "pcol"))
    return jax.shard_map(local, mesh=mesh, in_specs=in_specs, out_specs=out_specs, check_vma=False)
```
